512 devices in a mesh: tensor: 8 (over x, z_hi), seq: 64 (over z_lo, y, core).
Axes of the slice: x: 4, y: 8, z: 8 (z_hi: 2, z_lo: 4; z = z_hi * 4 + z_lo), core: 2. Of those that a mesh axis runs over, the one named last changes fastest.
Arguments:
- residual: bfloat16 [9728, 8192], P('seq', 'tensor'), may hold values from -6 to 6
- mean_vec: float32 [8192], replicated, may hold values from -6 to 6
- proj_u: float32 [8192], replicated, may hold values from -0.0625 to 0.0625
- proj_v: float32 [8192], replicated, may hold values from -6 to 6
- key_weight: bfloat16 [8192, 1024], P(None, 'tensor'), may hold values from -0.0625 to 0.0625
- value_weight: bfloat16 [8192, 1024], P(None, 'tensor'), may hold values from -0.0625 to 0.0625
- queries: bfloat16 [9728, 8192], P('seq', 'tensor'), may hold values from -110 to 110
- doc_ids: int32 [9728], P('seq'), may hold values from 0 to 3, never falling along the last dimension, each value on 1 to 4864 neighbouring positions
Outputs:
- attended: bfloat16 [9728, 8192], P('seq', 'tensor')
The draws below stay inside these ranges and needn't reach their ends.
Inputs may be any that keep to these rules, and one draw needn't show every extreme that they name: `doc_ids`: document numbers never fall along the sequence; every document has at least one token and the longest has exactly 4864.
All inputs are finite; a program needn't handle non-finite values.
Results may differ from the reference program's by a relative error of at most 0.014.
The reference program's roundings to bfloat16 on the way count: a program that leaves them out, or rounds other values in their place, can miss the bound.
Values may be sent and summed in bfloat16 or wider, within the bound.
A program may use at most 128 MiB of HBM per device.

```python
import math
import jax
import jax.numpy as jnp
import numpy as np
from jax import lax

MODEL_WIDTH = 8192
QUERY_HEADS = 64
KEY_VALUE_HEADS = 8
HEAD_SIZE = 128
TOKENS = 9728


def draw_queries(key, part):
    key = jax.random.fold_in(key, 7)
    second = jax.random.fold_in(key, 1)
    vals = jnp.clip(jax.random.normal(second, (TOKENS, QUERY_HEADS * HEAD_SIZE)), -6.0, 6.0)
    return vals.astype(jnp.float32).astype(jnp.bfloat16)


def shard_levels(key, extent, pieces, low, largest):
    def one(dim, blocks):
        heights = jax.random.uniform(jax.random.fold_in(jax.random.fold_in(key, 6), dim), (blocks,), jnp.float32, low / len(pieces), largest / len(pieces))
        return jnp.repeat(jnp.exp(heights), extent[dim] // blocks).reshape((-1,) + (1,) * (len(extent) - dim - 1))

    factor_of = one(*pieces[0])
    for cut in pieces[1:]:
        factor_of = factor_of * one(*cut)
    return factor_of


def split_up(count, total, bound, skew):
    portions = [(1 << 20) // math.isqrt(standing ** skew) + 1 for standing in range(2, count + 1)]
    surplus, given = total - bound - (count - 1), [1] * (count - 1)
    while surplus > 0:
        movable = [i for i in range(count - 1) if given[i] < bound]
        whole, left = sum([portions[i] for i in movable]), surplus
        for i in movable:
            more = min(bound - given[i], max(1, left * portions[i] // whole), surplus)
            given[i] = given[i] + more
            surplus = surplus - more
    return np.array([bound] + given)


def ragged_sizes(own_key, count, total, most, skew):
    if count == 2:
        one = jax.random.randint(own_key, (), max(1, total - most), min(most, total - 1) + 1)
        return jnp.stack([one, total - one])
    tallies = jnp.asarray(split_up(count, total, most, skew), jnp.int32)
    pairs = (count - 1) // 2
    donor, taker = tallies[1:1 + 2 * pairs:2], tallies[2:2 + 2 * pairs:2]
    slack = jnp.minimum(donor - 1, most - taker)
    shifted = jax.random.randint(jax.random.fold_in(own_key, 1), (pairs,), 0, 1 << 20) % (slack + 1)
    tallies = tallies.at[1:1 + 2 * pairs:2].set(donor - shifted).at[2:2 + 2 * pairs:2].set(taker + shifted)
    return tallies[jax.random.permutation(jax.random.fold_in(own_key, 2), count)]


def normal_values(key, dims, spread, reach, cuts=(), kind=jnp.bfloat16):
    drawn = jax.random.normal(key, dims, jnp.float32) * spread
    if len(cuts) > 0:
        drawn = shard_levels(key, dims, cuts, -0.22, 0.18) * drawn
    return jnp.clip(drawn, min=-reach, max=reach).astype(kind)


def setup_inputs(seed: int = 0) -> dict:
    streams_of = jax.random.split(jax.random.key(seed), 9)
    return {
        "residual": normal_values(streams_of[0], (TOKENS, MODEL_WIDTH), 1.0, 6.0, ((0, 64), (1, 8))),
        "mean_vec": normal_values(streams_of[1], (MODEL_WIDTH,), 1.0, 6.0, (), jnp.float32),
        "proj_u": normal_values(streams_of[2], (MODEL_WIDTH,), MODEL_WIDTH ** -0.5, 0.0625, (), jnp.float32),
        "proj_v": normal_values(streams_of[3], (MODEL_WIDTH,), 1.0, 6.0, (), jnp.float32),
        "key_weight": normal_values(streams_of[4], (MODEL_WIDTH, KEY_VALUE_HEADS * HEAD_SIZE), MODEL_WIDTH ** -0.5, 0.0625, ((1, 8),)),
        "value_weight": normal_values(streams_of[5], (MODEL_WIDTH, KEY_VALUE_HEADS * HEAD_SIZE), MODEL_WIDTH ** -0.5, 0.0625, ((1, 8),)),
        "queries": draw_queries(jax.random.fold_in(streams_of[8], 71), 0),
        "doc_ids": jnp.searchsorted(jnp.cumsum(ragged_sizes(streams_of[7], 4, TOKENS, TOKENS // 2, 0)), jnp.arange(TOKENS), side="right").astype(jnp.int32),
    }


def reference(residual, mean_vec, proj_u, proj_v, key_weight, value_weight, queries, doc_ids):
    whole = residual.astype(jnp.float32)
    coef = jnp.dot(whole - mean_vec[None, :], proj_u, precision=lax.Precision.HIGHEST)
    erased = (whole - coef[:, None] * proj_v[None, :]).astype(jnp.bfloat16)
    keys = jnp.dot(erased, key_weight, preferred_element_type=jnp.float32).astype(jnp.bfloat16)
    values = jnp.dot(erased, value_weight, preferred_element_type=jnp.float32).astype(jnp.bfloat16)
    position = jnp.arange(TOKENS, dtype=jnp.int32)
    allowed = (position[None, :] <= position[:, None]) & (doc_ids[None, :] == doc_ids[:, None])
    head_group = QUERY_HEADS // KEY_VALUE_HEADS
    scale = 1.0 / (HEAD_SIZE ** 0.5)

    def one_head(head):
        kv_head = head // head_group
        query = lax.dynamic_slice_in_dim(queries, head * HEAD_SIZE, HEAD_SIZE, 1)
        key = lax.dynamic_slice_in_dim(keys, kv_head * HEAD_SIZE, HEAD_SIZE, 1)
        value = lax.dynamic_slice_in_dim(values, kv_head * HEAD_SIZE, HEAD_SIZE, 1)
        score = jnp.dot(query, key.T, preferred_element_type=jnp.float32) * scale
        score = jnp.where(allowed, score, -jnp.inf)
        top = jnp.max(score, axis=1, keepdims=True)
        expo = jnp.exp(score - top)
        total = jnp.sum(expo, axis=1)
        mixed = jnp.dot(expo.astype(jnp.bfloat16), value, preferred_element_type=jnp.float32)
        return (mixed / total[:, None]).astype(jnp.bfloat16)

    heads = lax.map(one_head, jnp.arange(QUERY_HEADS, dtype=jnp.int32))
    return jnp.transpose(heads, (1, 0, 2)).reshape(TOKENS, QUERY_HEADS * HEAD_SIZE)
```

```python
import functools
import jax
import jax.numpy as jnp
from jax import lax
from jax.experimental import pallas as pl
from jax.experimental.pallas import tpu as pltpu
from jax.sharding import PartitionSpec as P

HEADS = 8
HEAD = 128
TOK = 152
ROWS = 160
CUT = ((0, 80), (80, 80))
WIDTH = 1024
YN = 8
SCALE = 1.0 / HEAD**0.5
FAR = -1e30
MESH = pl.DeviceIdType.MESH
OWN, MATE = 4 * YN, 4 * YN + 1
SLOTS = 4 * YN + 2
SEMS = 96


def kernel(
    res, mean, read, drop, wk_hbm, wv_hbm, qry, doc, out,
    rbuf, wbuf, kvbuf, qbuf, kx, vx, acc, top, ssem, rsem, wsem,
):
    t = lax.axis_index("tensor")
    s = lax.axis_index("seq")
    x, zh = t // 2, t % 2
    zl, y, core = s // 16, (s // 2) % YN, s % 2

    def dev(x_, zh_, zl_, y_, core_):
        return (x_ * 2 + zh_, zl_ * 16 + y_ * 2 + core_)

    right = dev((x + 1) % 4, zh, zl, y, core)
    left = dev((x + 3) % 4, zh, zl, y, core)
    across = dev(x, 1 - zh, zl, y, core)
    above = dev(x, zh, (zl + 1) % 4, y, core)
    below = dev(x, zh, (zl + 3) % 4, y, core)
    mate = dev(x, zh, zl, y, 1 - core)
    has_above, has_below = zl < 3, zl > 0

    def ring(d):
        return dev(x, zh, zl, (y + d) % YN, core)

    bar = pltpu.get_barrier_semaphore()

    def hello(device):
        pl.semaphore_signal(bar, inc=1, device_id=device, device_id_type=MESH)

    for device in [right, left, across, mate] + [ring(d) for d in range(1, YN)]:
        hello(device)

    @pl.when(has_above)
    def _():
        hello(above)

    @pl.when(has_below)
    def _():
        hello(below)

    wcopies = [
        pltpu.make_async_copy(wk_hbm, wbuf.at[:, pl.ds(0, HEAD)], wsem.at[0]),
        pltpu.make_async_copy(wv_hbm, wbuf.at[:, pl.ds(HEAD, HEAD)], wsem.at[1]),
    ]
    for cp in wcopies:
        cp.start()

    def padded(value):
        wide = value.astype(jnp.float32)
        tail = jnp.zeros((ROWS - TOK, wide.shape[1]), jnp.float32)
        return jnp.concatenate([wide, tail], axis=0).astype(jnp.bfloat16)

    rbuf[0] = padded(res[...])
    lane = lax.broadcasted_iota(jnp.int32, (1, HEAD), 1)
    docs = doc[...]
    low = jnp.zeros((1, HEAD), jnp.float32)
    high = jnp.zeros((1, HEAD), jnp.float32)
    for d in range(4):
        under = jnp.sum((docs < d).astype(jnp.float32), axis=1, keepdims=True)
        upto = jnp.sum((docs <= d).astype(jnp.float32), axis=1, keepdims=True)
        low = jnp.where(lane == d, under, low)
        high = jnp.where(lane == d, upto, high)
    row_at = lax.broadcasted_iota(jnp.int32, (ROWS, HEAD), 0).astype(jnp.float32)
    inside = (row_at >= low) & (row_at < high)
    q_mark = jnp.where(inside, FAR, 0.0).astype(jnp.bfloat16)
    for h in range(HEADS):
        qbuf[h, :, 0:HEAD] = padded(qry[:, h * HEAD:(h + 1) * HEAD])
        qbuf[h, :, HEAD:2 * HEAD] = q_mark
    empty = jnp.zeros((ROWS, 2 * HEAD), jnp.bfloat16)

    @pl.when(core == 0)
    def _():
        kvbuf[MATE] = empty

    @pl.when(zl == 0)
    def _():
        kvbuf[0] = empty
        for d in range(YN):
            kvbuf[4 * d + 1] = empty

    vx[:, HEAD:2 * HEAD] = jnp.ones((4 * ROWS, HEAD), jnp.bfloat16)

    peers = 4 + YN - 1 + jnp.where(has_above, 1, 0) + jnp.where(has_below, 1, 0)
    pl.semaphore_wait(bar, peers)

    used = [0]
    sent = []

    def copy(buf, src, dst, cut, device):
        i = used[0]
        used[0] += 1
        first, rows = cut
        return pltpu.make_async_remote_copy(
            src_ref=buf.at[src, pl.ds(first, rows)],
            dst_ref=buf.at[dst, pl.ds(first, rows)],
            send_sem=ssem.at[i],
            recv_sem=rsem.at[i],
            device_id=device,
            device_id_type=MESH,
        )

    def go(cp, when=None):
        sent.append((cp, when))
        if when is None:
            cp.start()
        else:
            pl.when(when)(cp.start)

    def got(cp, when=None):
        if when is None:
            cp.wait_recv()
        else:
            pl.when(when)(cp.wait_recv)

    over = [copy(rbuf, 0, 4, cut, across) for cut in CUT]
    to_right = [[copy(rbuf, 4 * h, 4 * h + 1, cut, right) for cut in CUT] for h in range(2)]
    to_left = [[copy(rbuf, 4 * h, 4 * h + 2, cut, left) for cut in CUT] for h in range(2)]
    onward = [
        [copy(rbuf, 4 * h + 1, 4 * h + 3, CUT[0], right), copy(rbuf, 4 * h + 2, 4 * h + 3, CUT[1], left)]
        for h in range(2)
    ]
    for c in range(2):
        go(over[c])
    for c in range(2):
        go(to_right[0][c])
        go(to_left[0][c])
    got(to_right[0][0])
    go(onward[0][0])
    got(to_left[0][0])
    got(to_left[0][1])
    go(onward[0][1])
    got(to_right[0][1])
    for c in range(2):
        got(over[c])
        go(to_right[1][c])
        go(to_left[1][c])
    got(onward[0][0])
    got(onward[0][1])
    got(to_right[1][0])
    go(onward[1][0])
    got(to_left[1][0])

    whose = [(x * 2 + zh), ((x + 3) % 4) * 2 + zh, ((x + 1) % 4) * 2 + zh, ((x + 2) % 4) * 2 + zh]
    whose = whose + [w + 1 - 2 * zh for w in whose]

    def project(c):
        first, rows = CUT[c]
        part = jnp.zeros((rows, HEAD), jnp.float32)
        for slot in range(8):
            block = rbuf[slot, first:first + rows, :].astype(jnp.float32)
            term = (block - mean[whose[slot]]) * read[whose[slot]]
            for j in range(WIDTH // HEAD):
                part = part + term[:, j * HEAD:(j + 1) * HEAD]
        coef = jnp.sum(part, axis=1, keepdims=True)
        total = jnp.zeros((rows, 2 * HEAD), jnp.float32)
        for slot in range(8):
            block = rbuf[slot, first:first + rows, :].astype(jnp.float32)
            erased = (block - coef * drop[whose[slot]]).astype(jnp.bfloat16)
            weight = wbuf[pl.ds(pl.multiple_of(whose[slot] * WIDTH, WIDTH), WIDTH), :]
            total = total + jnp.dot(erased, weight, preferred_element_type=jnp.float32)
        if first + rows > TOK:
            at = lax.broadcasted_iota(jnp.int32, (rows, 2 * HEAD), 0) + first
            blank = jnp.zeros((1, HEAD), jnp.float32)
            low2 = jnp.concatenate([low, blank], axis=1)
            high2 = jnp.concatenate([high, blank], axis=1)
            total = jnp.where(at >= TOK, jnp.where(at == TOK, low2, jnp.where(at == TOK + 1, high2, 0.0)), total)
        kvbuf[OWN, first:first + rows, :] = total.astype(jnp.bfloat16)

    up = [copy(kvbuf, OWN, 0, cut, above) for cut in CUT]
    up2 = [copy(kvbuf, 0, 1, cut, above) for cut in CUT]
    near = [
        [copy(kvbuf, jnp.where(y + d < YN, OWN, 0), 4 * d, cut, ring(d)) for cut in CUT]
        for d in range(1, YN)
    ]
    far = [[copy(kvbuf, 4 * d, 4 * d + 1, cut, above) for cut in CUT] for d in range(1, YN)]
    side = [copy(kvbuf, OWN, MATE, cut, mate) for cut in CUT]
    used_side = [used[0]]

    def pair(d, c):
        i = used[0]
        used[0] += 1
        first, rows = CUT[c]
        return pltpu.make_async_remote_copy(
            src_ref=kvbuf.at[pl.ds(4 * d, 2), pl.ds(first, rows)],
            dst_ref=kvbuf.at[pl.ds(4 * d + 2, 2), pl.ds(first, rows)],
            send_sem=ssem.at[i],
            recv_sem=rsem.at[i],
            device_id=mate,
            device_id_type=MESH,
        )

    pairs = [[pair(d, c) for c in range(2)] for d in range(YN)]
    order = sorted(range(1, YN), key=lambda d: min(d, YN - d))

    def share(c):
        go(up[c], has_above)
        for d in order:
            go(near[d - 1][c], y + d < YN)
        go(side[c], core == 0)

    def wrapped(c):
        got(up[c], has_below)
        go(up2[c], has_above)
        for d in order:
            go(near[d - 1][c], y + d >= YN)

    def relay(c, d):
        got(near[d - 1][c])
        go(far[d - 1][c], has_above)

    for cp in wcopies:
        cp.wait()
    got(onward[1][0])
    project(0)
    share(0)
    got(to_left[1][1])
    go(onward[1][1])
    got(to_right[1][1])
    wrapped(0)
    got(onward[1][1])
    project(1)
    share(1)
    for d in order:
        relay(0, d)
    wrapped(1)
    for c in range(2):
        got(up2[c], has_below)
        go(pairs[0][c])

    def attend(slot0, blocks, start):
        keys = blocks * ROWS
        for i in range(blocks):
            rows = slice(i * ROWS, (i + 1) * ROWS)
            block = kvbuf[slot0 + i]
            kx[rows, 0:HEAD] = block[:, 0:HEAD]
            vx[rows, 0:HEAD] = block[:, HEAD:2 * HEAD]
            tail = kvbuf[slot0 + i, 144:160, 0:HEAD].astype(jnp.float32)
            seen = (row_at >= tail[8:9]) & (row_at < tail[9:10])
            kx[rows, HEAD:2 * HEAD] = jnp.where(seen, 0.0, 1.0).astype(jnp.bfloat16)

        def one(h, carry):
            score = lax.dot_general(
                qbuf[h], kx[0:keys], (((1,), (1,)), ((), ())), preferred_element_type=jnp.float32
            )
            if start:
                q_at = lax.broadcasted_iota(jnp.int32, (ROWS, keys), 0)
                k_at = lax.broadcasted_iota(jnp.int32, (ROWS, keys), 1)
                score = jnp.where((k_at <= q_at) | (k_at >= ROWS), score, FAR)
            best = jnp.max(score, axis=1, keepdims=True)
            if not start:
                old = top[h][:, 0:1]
                best = jnp.maximum(best, old)
            expo = jnp.exp((score - best) * SCALE).astype(jnp.bfloat16)
            mixed = jnp.dot(expo, vx[0:keys], preferred_element_type=jnp.float32)
            if not start:
                mixed = mixed + acc[h] * jnp.exp((old - best) * SCALE)
            acc[h] = mixed
            top[h] = jnp.broadcast_to(best, (ROWS, HEAD))
            return carry

        lax.fori_loop(0, HEADS, one, 0)

    for c in range(2):
        got(side[c], core == 1)
    attend(OWN, 2, True)
    for d in order:
        relay(1, d)
        for c in range(2):
            got(far[d - 1][c], has_below)
            go(pairs[d][c])
    for c in range(2):
        got(pairs[0][c])
    attend(0, 4, False)
    for d in order:
        for c in range(2):
            got(pairs[d][c])
        attend(4 * d, 4, False)

    for h in range(HEADS):
        both = acc[h]
        out[:, h * HEAD:(h + 1) * HEAD] = (both[0:TOK, 0:HEAD] / both[0:TOK, HEAD:2 * HEAD]).astype(jnp.bfloat16)

    for cp, when in sent:
        if when is None:
            cp.wait_send()
        else:
            pl.when(when)(cp.wait_send)


def on_device(residual, mean_vec, proj_u, proj_v, key_weight, value_weight, queries, doc_ids):
    whole = pl.BlockSpec(memory_space=pltpu.VMEM)
    hbm = pl.BlockSpec(memory_space=pl.ANY)
    flat = (8, 1, WIDTH)
    return pl.pallas_call(
        kernel,
        out_shape=jax.ShapeDtypeStruct((TOK, WIDTH), jnp.bfloat16),
        in_specs=[whole, whole, whole, whole, hbm, hbm, whole, whole],
        out_specs=whole,
        scratch_shapes=[
            pltpu.VMEM((8, ROWS, WIDTH), jnp.bfloat16),
            pltpu.VMEM((8 * WIDTH, 2 * HEAD), jnp.bfloat16),
            pltpu.VMEM((SLOTS, ROWS, 2 * HEAD), jnp.bfloat16),
            pltpu.VMEM((HEADS, ROWS, 2 * HEAD), jnp.bfloat16),
            pltpu.VMEM((4 * ROWS, 2 * HEAD), jnp.bfloat16),
            pltpu.VMEM((4 * ROWS, 2 * HEAD), jnp.bfloat16),
            pltpu.VMEM((HEADS, ROWS, 2 * HEAD), jnp.float32),
            pltpu.VMEM((HEADS, ROWS, HEAD), jnp.float32),
            pltpu.SemaphoreType.DMA((SEMS,)),
            pltpu.SemaphoreType.DMA((SEMS,)),
            pltpu.SemaphoreType.DMA((2,)),
        ],
        compiler_params=pltpu.CompilerParams(
            collective_id=0, has_side_effects=True, vmem_limit_bytes=48 << 20
        ),
    )(
        residual, mean_vec.reshape(flat), proj_u.reshape(flat), proj_v.reshape(flat),
        key_weight, value_weight, queries, doc_ids.reshape(1, TOK),
    )


def solution(mesh):
    return jax.shard_map(
        on_device,
        mesh=mesh,
        in_specs=(
            P("seq", "tensor"), P(), P(), P(), P(None, "tensor"), P(None, "tensor"),
            P("seq", "tensor"), P("seq"),
        ),
        out_specs=P("seq", "tensor"),
        check_vma=False,
    )
```

```python
import functools
import jax
import jax.numpy as jnp
from jax import lax
from jax.experimental import pallas as pl
from jax.experimental.pallas import tpu as pltpu
from jax.sharding import PartitionSpec as P

HEADS = 8
HEAD = 128
TOK = 152
ROWS = 160
GAP = 72
CUT = ((0, 80), (80, 80))
PIECE = ((0, 48), (48, 32), (80, 48), (128, 32))
WIDTH = 1024
YN = 8
SCALE = 1.0 / HEAD**0.5
LOG2E = 1.4426950408889634
FAR = -1e30
MESH = pl.DeviceIdType.MESH
OWN, MATE = 4 * YN, 4 * YN + 1
SLOTS = 4 * YN + 2
SEMS = 96


def kernel(
    res_hbm, mean_hbm, read_hbm, drop_hbm, wk_hbm, wv_hbm, qry_hbm, doc_hbm, out,
    res, mean, read, drop, qry, doc,
    rbuf, wbuf, kvbuf, qbuf, kx, vx, acc, top, ssem, rsem, wsem,
):
    t = lax.axis_index("tensor")
    s = lax.axis_index("seq")
    x, zh = t // 2, t % 2
    zl, y, core = s // 16, (s // 2) % YN, s % 2

    def dev(x_, zh_, zl_, y_, core_):
        return (x_ * 2 + zh_, zl_ * 16 + y_ * 2 + core_)

    right = dev((x + 1) % 4, zh, zl, y, core)
    left = dev((x + 3) % 4, zh, zl, y, core)
    across = dev(x, 1 - zh, zl, y, core)
    above = dev(x, zh, (zl + 1) % 4, y, core)
    below = dev(x, zh, (zl + 3) % 4, y, core)
    mate = dev(x, zh, zl, y, 1 - core)
    has_above, has_below = zl < 3, zl > 0

    def ring(d):
        return dev(x, zh, zl, (y + d) % YN, core)

    bar = pltpu.get_barrier_semaphore()

    def hello(device):
        pl.semaphore_signal(bar, inc=1, device_id=device, device_id_type=MESH)

    for device in [right, left, across, mate] + [ring(d) for d in range(1, YN)]:
        hello(device)

    @pl.when(has_above)
    def _():
        hello(above)

    @pl.when(has_below)
    def _():
        hello(below)

    loads = [
        pltpu.make_async_copy(src, dst, wsem.at[i])
        for i, (src, dst) in enumerate([
            (res_hbm, res), (doc_hbm, doc), (qry_hbm, qry), (mean_hbm, mean), (read_hbm, read), (drop_hbm, drop),
            (wk_hbm, wbuf.at[:, pl.ds(0, HEAD)]), (wv_hbm, wbuf.at[:, pl.ds(HEAD, HEAD)]),
        ])
    ]
    for cp in loads:
        cp.start()

    def padded(value):
        wide = value.astype(jnp.float32)
        blank = jnp.zeros((ROWS - TOK, wide.shape[1]), jnp.float32)
        return jnp.concatenate([wide[:GAP], blank, wide[GAP:]], axis=0).astype(jnp.bfloat16)

    empty = jnp.zeros((ROWS, 2 * HEAD), jnp.bfloat16)

    @pl.when(core == 0)
    def _():
        kvbuf[MATE] = empty

    @pl.when(zl == 0)
    def _():
        kvbuf[0] = empty
        for d in range(YN):
            kvbuf[4 * d + 1] = empty

    loads[0].wait()
    rbuf[0] = padded(res[...])

    peers = 4 + YN - 1 + jnp.where(has_above, 1, 0) + jnp.where(has_below, 1, 0)
    pl.semaphore_wait(bar, peers)

    used = [0]
    sent = []

    def copy(buf, src, dst, cut, device):
        i = used[0]
        used[0] += 1
        first, rows = cut
        return pltpu.make_async_remote_copy(
            src_ref=buf.at[src, pl.ds(first, rows)],
            dst_ref=buf.at[dst, pl.ds(first, rows)],
            send_sem=ssem.at[i],
            recv_sem=rsem.at[i],
            device_id=device,
            device_id_type=MESH,
        )

    def go(cp, when=None):
        sent.append((cp, when))
        if when is None:
            cp.start()
        else:
            pl.when(when)(cp.start)

    def got(cp, when=None):
        if when is None:
            cp.wait_recv()
        else:
            pl.when(when)(cp.wait_recv)

    over = [copy(rbuf, 0, 4, cut, across) for cut in PIECE]
    to_right = [[copy(rbuf, 4 * h, 4 * h + 1, cut, right) for cut in (CUT, PIECE)[h]] for h in range(2)]
    to_left = [[copy(rbuf, 4 * h, 4 * h + 2, cut, left) for cut in (CUT, PIECE)[h]] for h in range(2)]
    rightward = ((True, False), (True, False, False, True))
    onward = [
        [
            copy(rbuf, 4 * h + 1, 4 * h + 3, cut, right) if way else copy(rbuf, 4 * h + 2, 4 * h + 3, cut, left)
            for way, cut in zip(rightward[h], (CUT, PIECE)[h])
        ]
        for h in range(2)
    ]

    def spread(h, p):
        go(to_right[h][p])
        go(to_left[h][p])

    def carry_on(h, p):
        got((to_right if rightward[h][p] else to_left)[h][p])
        go(onward[h][p])

    def rest(h, p):
        got((to_left if rightward[h][p] else to_right)[h][p])
        got(onward[h][p])

    go(over[0])
    spread(0, 0)
    go(over[1])
    spread(0, 1)
    for cp in loads[1:3]:
        cp.wait()
    lane = lax.broadcasted_iota(jnp.int32, (1, HEAD), 1)
    docs = doc[...]
    low = jnp.zeros((1, HEAD), jnp.float32)
    high = jnp.zeros((1, HEAD), jnp.float32)
    for d in range(4):
        under = jnp.sum((docs < d).astype(jnp.float32), axis=1, keepdims=True)
        upto = jnp.sum((docs <= d).astype(jnp.float32), axis=1, keepdims=True)
        low = jnp.where(lane == d, under, low)
        high = jnp.where(lane == d, upto, high)
    low = jnp.where(low >= GAP, low + (ROWS - TOK), low)
    high = jnp.where(high > GAP, high + (ROWS - TOK), high)
    row_at = lax.broadcasted_iota(jnp.int32, (ROWS, HEAD), 0).astype(jnp.float32)
    token = (row_at < GAP) | (row_at >= GAP + ROWS - TOK)
    inside = (row_at >= low) & (row_at < high) & token
    q_mark = jnp.where(inside, FAR, 0.0).astype(jnp.bfloat16)
    for h in range(HEADS):
        qbuf[h, :, 0:HEAD] = padded(qry[:, h * HEAD:(h + 1) * HEAD])
        qbuf[h, :, HEAD:2 * HEAD] = q_mark
    vx[:, HEAD:2 * HEAD] = jnp.ones((4 * ROWS, HEAD), jnp.bfloat16)
    for cp in loads[3:]:
        cp.wait()

    carry_on(0, 0)
    got(over[0])
    go(over[2])
    spread(1, 0)
    carry_on(0, 1)
    got(over[1])
    go(over[3])
    spread(1, 1)
    carry_on(1, 0)
    got(over[2])
    spread(1, 2)
    carry_on(1, 1)
    got(over[3])
    spread(1, 3)

    whose = [(x * 2 + zh), ((x + 3) % 4) * 2 + zh, ((x + 1) % 4) * 2 + zh, ((x + 2) % 4) * 2 + zh]
    whose = whose + [w + 1 - 2 * zh for w in whose]

    def project(c):
        first, rows = CUT[c]
        part = jnp.zeros((rows, HEAD), jnp.float32)
        for slot in range(8):
            block = rbuf[slot, first:first + rows, :].astype(jnp.float32)
            term = (block - mean[whose[slot]]) * read[whose[slot]]
            for j in range(WIDTH // HEAD):
                part = part + term[:, j * HEAD:(j + 1) * HEAD]
        coef = jnp.sum(part, axis=1, keepdims=True)
        total = jnp.zeros((rows, 2 * HEAD), jnp.float32)
        for slot in range(8):
            block = rbuf[slot, first:first + rows, :].astype(jnp.float32)
            erased = (block - coef * drop[whose[slot]]).astype(jnp.bfloat16)
            weight = wbuf[pl.ds(pl.multiple_of(whose[slot] * WIDTH, WIDTH), WIDTH), :]
            total = total + jnp.dot(erased, weight, preferred_element_type=jnp.float32)
        if first == 0:
            at = lax.broadcasted_iota(jnp.int32, (rows, 2 * HEAD), 0)
            blank = jnp.zeros((1, HEAD), jnp.float32)
            low2 = jnp.concatenate([low, blank], axis=1)
            high2 = jnp.concatenate([high, blank], axis=1)
            total = jnp.where(at >= GAP, jnp.where(at == GAP, low2, jnp.where(at == GAP + 1, high2, 0.0)), total)
        kvbuf[OWN, first:first + rows, :] = total.astype(jnp.bfloat16)

    up = [copy(kvbuf, OWN, 0, cut, above) for cut in CUT]
    up2 = [copy(kvbuf, 0, 1, cut, above) for cut in CUT]
    near = [
        [copy(kvbuf, jnp.where(y + d < YN, OWN, 0), 4 * d, cut, ring(d)) for cut in CUT]
        for d in range(1, YN)
    ]
    far = [[copy(kvbuf, 4 * d, 4 * d + 1, cut, above) for cut in CUT] for d in range(1, YN)]
    side = [copy(kvbuf, OWN, MATE, cut, mate) for cut in CUT]
    used_side = [used[0]]

    def pair(d, c):
        i = used[0]
        used[0] += 1
        first, rows = CUT[c]
        return pltpu.make_async_remote_copy(
            src_ref=kvbuf.at[pl.ds(4 * d, 2), pl.ds(first, rows)],
            dst_ref=kvbuf.at[pl.ds(4 * d + 2, 2), pl.ds(first, rows)],
            send_sem=ssem.at[i],
            recv_sem=rsem.at[i],
            device_id=mate,
            device_id_type=MESH,
        )

    pairs = [[pair(d, c) for c in range(2)] for d in range(YN)]
    order = sorted(range(1, YN), key=lambda d: min(d, YN - d))

    def share(c):
        go(up[c], has_above)
        for d in order:
            go(near[d - 1][c], y + d < YN)
        go(side[c], core == 0)

    def wrapped(c):
        got(up[c], has_below)
        go(up2[c], has_above)
        for d in order:
            go(near[d - 1][c], y + d >= YN)

    def relay(c, d):
        got(near[d - 1][c])
        go(far[d - 1][c], has_above)

    rest(0, 0)
    rest(1, 0)
    rest(1, 1)
    carry_on(1, 2)
    project(0)
    share(0)
    carry_on(1, 3)
    wrapped(0)
    rest(0, 1)
    rest(1, 2)
    rest(1, 3)
    project(1)
    share(1)
    def attend(blocks, start=False):
        keys = sum(rows for _, (_, rows) in blocks)
        at = 0
        for slot, (first, rows) in blocks:
            put = slice(at, at + rows)
            at += rows
            block = kvbuf[slot, first:first + rows, :]
            kx[put, 0:HEAD] = block[:, 0:HEAD]
            vx[put, 0:HEAD] = block[:, HEAD:2 * HEAD]
            mark = kvbuf[slot, GAP - 8:GAP + 8, 0:HEAD].astype(jnp.float32)
            here = slice(first, first + rows)
            seen = (row_at[here] >= mark[8:9]) & (row_at[here] < mark[9:10]) & token[here]
            kx[put, HEAD:2 * HEAD] = jnp.where(seen, 0.0, 1.0).astype(jnp.bfloat16)

        score = lax.dot_general(
            qbuf[...].reshape(HEADS * ROWS, 2 * HEAD), kx[0:keys], (((1,), (1,)), ((), ())),
            preferred_element_type=jnp.float32,
        )
        if start:
            shape = (HEADS, ROWS, keys)
            q_at = lax.broadcasted_iota(jnp.int32, shape, 1).reshape(HEADS * ROWS, keys)
            k_at = lax.broadcasted_iota(jnp.int32, shape, 2).reshape(HEADS * ROWS, keys)
            score = jnp.where((k_at <= q_at) | (k_at >= ROWS), score, FAR)
        tiles = [score[:, i:i + HEAD] for i in range(0, keys, HEAD)]
        rough = functools.reduce(jnp.maximum, tiles[1:], tiles[0]) if keys % HEAD == 0 else score
        best = jnp.max(rough, axis=1, keepdims=True)
        if start:
            best = jnp.broadcast_to(best, (HEADS * ROWS, HEAD))
            expo = jnp.exp2((score - best[:, 0:1]) * (SCALE * LOG2E)).astype(jnp.bfloat16)
        else:
            old = top[...]
            best = jnp.maximum(best, old)
            wide = jnp.concatenate([best] * len(tiles), axis=1)
            expo = jnp.exp2((score - wide) * (SCALE * LOG2E)).astype(jnp.bfloat16)
        mixed = jnp.dot(expo, vx[0:keys], preferred_element_type=jnp.float32)
        if not start:
            factor = jnp.exp2((old - best) * (SCALE * LOG2E))
            mixed = mixed + acc[...] * jnp.concatenate([factor, factor], axis=1)
        acc[...] = mixed
        top[...] = best

    calls = ((0, 1), (YN - 1, 2), (YN - 2, 3), (YN - 3, 4))

    def to_mate(c, n):
        for d in calls[n]:
            if d == 0:
                got(up2[c], has_below)
            else:
                got(far[d - 1][c], has_below)
            go(pairs[d][c])

    def take(c, n):
        for d in calls[n]:
            got(pairs[d][c])
        attend([(4 * d + j, CUT[c]) for d in calls[n] for j in range(4)])

    for d in order:
        relay(0, d)
    wrapped(1)
    to_mate(0, 0)
    for c in range(2):
        got(side[c], core == 1)
    attend([(OWN, (0, ROWS)), (MATE, (0, ROWS))], True)
    to_mate(0, 1)
    take(0, 0)
    to_mate(0, 2)
    relay(1, order[0])
    relay(1, order[1])
    take(0, 1)
    to_mate(0, 3)
    relay(1, order[2])
    relay(1, order[3])
    take(0, 2)
    for d in order[4:]:
        relay(1, d)
    to_mate(1, 0)
    take(0, 3)
    for n in range(4):
        if n < 3:
            to_mate(1, n + 1)
        take(1, n)

    for h in range(HEADS):
        both = acc[h * ROWS:(h + 1) * ROWS]
        mean_value = (both[:, 0:HEAD] / both[:, HEAD:2 * HEAD])
        kept = jnp.concatenate([mean_value[:GAP], mean_value[GAP + ROWS - TOK:]], axis=0)
        out[:, h * HEAD:(h + 1) * HEAD] = kept.astype(jnp.bfloat16)

    for cp, when in sent:
        if when is None:
            cp.wait_send()
        else:
            pl.when(when)(cp.wait_send)


def on_device(residual, mean_vec, proj_u, proj_v, key_weight, value_weight, queries, doc_ids):
    whole = pl.BlockSpec(memory_space=pltpu.VMEM)
    hbm = pl.BlockSpec(memory_space=pltpu.HBM)
    flat = (8, 1, WIDTH)
    return pl.pallas_call(
        kernel,
        out_shape=jax.ShapeDtypeStruct((TOK, WIDTH), jnp.bfloat16),
        in_specs=[hbm] * 8,
        out_specs=whole,
        scratch_shapes=[
            pltpu.VMEM((TOK, WIDTH), jnp.bfloat16),
            pltpu.VMEM(flat, jnp.float32),
            pltpu.VMEM(flat, jnp.float32),
            pltpu.VMEM(flat, jnp.float32),
            pltpu.VMEM((TOK, WIDTH), jnp.bfloat16),
            pltpu.VMEM((1, TOK), jnp.int32),
            pltpu.VMEM((8, ROWS, WIDTH), jnp.bfloat16),
            pltpu.VMEM((8 * WIDTH, 2 * HEAD), jnp.bfloat16),
            pltpu.VMEM((SLOTS, ROWS, 2 * HEAD), jnp.bfloat16),
            pltpu.VMEM((HEADS, ROWS, 2 * HEAD), jnp.bfloat16),
            pltpu.VMEM((4 * ROWS, 2 * HEAD), jnp.bfloat16),
            pltpu.VMEM((4 * ROWS, 2 * HEAD), jnp.bfloat16),
            pltpu.VMEM((HEADS * ROWS, 2 * HEAD), jnp.float32),
            pltpu.VMEM((HEADS * ROWS, HEAD), jnp.float32),
            pltpu.SemaphoreType.DMA((SEMS,)),
            pltpu.SemaphoreType.DMA((SEMS,)),
            pltpu.SemaphoreType.DMA((8,)),
        ],
        compiler_params=pltpu.CompilerParams(
            collective_id=0, has_side_effects=True, vmem_limit_bytes=60 << 20
        ),
    )(
        residual, mean_vec.reshape(flat), proj_u.reshape(flat), proj_v.reshape(flat),
        key_weight, value_weight, queries, doc_ids.reshape(1, TOK),
    )


def solution(mesh):
    return jax.shard_map(
        on_device,
        mesh=mesh,
        in_specs=(
            P("seq", "tensor"), P(), P(), P(), P(None, "tensor"), P(None, "tensor"),
            P("seq", "tensor"), P("seq"),
        ),
        out_specs=P("seq", "tensor"),
        check_vma=False,
    )
```

```python
import functools
import jax
import jax.numpy as jnp
from jax import lax
from jax.experimental import pallas as pl
from jax.experimental.pallas import tpu as pltpu
from jax.sharding import PartitionSpec as P

HEADS = 8
HEAD = 128
TOK = 152
ROWS = 160
GAP = 40
CUT = ((0, 48), (48, 64), (112, 48))
WIDTH = 1024
YN = 8
SCALE = 1.0 / HEAD**0.5
LOG2E = 1.4426950408889634
FAR = -1e30
MESH = pl.DeviceIdType.MESH
OWN, MATE = 4 * YN, 4 * YN + 1
SLOTS = 4 * YN + 2
SEMS = 112
KEYS = 1024


def kernel(
    res_hbm, mean_hbm, read_hbm, drop_hbm, wk_hbm, wv_hbm, qry_hbm, doc_hbm, out,
    res, mean, read, drop, qry, doc,
    rbuf, wbuf, kvbuf, qbuf, kx, vx, acc, top, ssem, rsem, wsem,
):
    t = lax.axis_index("tensor")
    s = lax.axis_index("seq")
    x, zh = t // 2, t % 2
    zl, y, core = s // 16, (s // 2) % YN, s % 2

    def dev(x_, zh_, zl_, y_, core_):
        return (x_ * 2 + zh_, zl_ * 16 + y_ * 2 + core_)

    right = dev((x + 1) % 4, zh, zl, y, core)
    left = dev((x + 3) % 4, zh, zl, y, core)
    facing = dev((x + 2) % 4, zh, zl, y, core)
    across = dev(x, 1 - zh, zl, y, core)
    above = dev(x, zh, (zl + 1) % 4, y, core)
    below = dev(x, zh, (zl + 3) % 4, y, core)
    mate = dev(x, zh, zl, y, 1 - core)
    has_above, has_below = zl < 3, zl > 0

    def ring(d):
        return dev(x, zh, zl, (y + d) % YN, core)

    bar = pltpu.get_barrier_semaphore()

    def hello(device):
        pl.semaphore_signal(bar, inc=1, device_id=device, device_id_type=MESH)

    for device in [right, left, facing, across, mate] + [ring(d) for d in range(1, YN)]:
        hello(device)

    @pl.when(has_above)
    def _():
        hello(above)

    @pl.when(has_below)
    def _():
        hello(below)

    loads = [
        pltpu.make_async_copy(src, dst, wsem.at[i])
        for i, (src, dst) in enumerate([
            (res_hbm, res), (doc_hbm, doc), (qry_hbm, qry), (mean_hbm, mean), (read_hbm, read), (drop_hbm, drop),
            (wk_hbm, wbuf.at[:, pl.ds(0, HEAD)]), (wv_hbm, wbuf.at[:, pl.ds(HEAD, HEAD)]),
        ])
    ]
    for cp in loads:
        cp.start()

    def padded(value):
        wide = value.astype(jnp.float32)
        blank = jnp.zeros((ROWS - TOK, wide.shape[1]), jnp.float32)
        return jnp.concatenate([wide[:GAP], blank, wide[GAP:]], axis=0).astype(jnp.bfloat16)

    empty = jnp.zeros((ROWS, 2 * HEAD), jnp.bfloat16)

    @pl.when(core == 0)
    def _():
        kvbuf[MATE] = empty

    @pl.when(zl == 0)
    def _():
        kvbuf[0] = empty
        for d in range(YN):
            kvbuf[4 * d + 1] = empty

    loads[0].wait()
    rbuf[0] = padded(res[...])

    peers = 5 + YN - 1 + jnp.where(has_above, 1, 0) + jnp.where(has_below, 1, 0)
    pl.semaphore_wait(bar, peers)

    used = [0]
    sent = []

    def copy(buf, src, dst, cut, device):
        i = used[0]
        used[0] += 1
        first, rows = cut
        return pltpu.make_async_remote_copy(
            src_ref=buf.at[src, pl.ds(first, rows)],
            dst_ref=buf.at[dst, pl.ds(first, rows)],
            send_sem=ssem.at[i],
            recv_sem=rsem.at[i],
            device_id=device,
            device_id_type=MESH,
        )

    def go(cp, when=None):
        sent.append((cp, when))
        if when is None:
            cp.start()
        else:
            pl.when(when)(cp.start)

    def got(cp, when=None):
        if when is None:
            cp.wait_recv()
        else:
            pl.when(when)(cp.wait_recv)

    over = [copy(rbuf, 0, 4, cut, across) for cut in CUT]
    to_right = [[copy(rbuf, 4 * h, 4 * h + 1, cut, right) for cut in CUT] for h in range(2)]
    to_left = [[copy(rbuf, 4 * h, 4 * h + 2, cut, left) for cut in CUT] for h in range(2)]
    rightward = ((True, False, False), (False, True, True))
    onward = [
        [
            copy(rbuf, 4 * h + 1, 4 * h + 3, cut, right) if way else copy(rbuf, 4 * h + 2, 4 * h + 3, cut, left)
            for way, cut in zip(rightward[h], CUT)
        ]
        for h in range(2)
    ]

    hop2 = [[copy(rbuf, 4 * h, 4 * h + 3, cut, facing) for cut in CUT] for h in range(2)]
    is_direct = ((False, False, False), (True, True, True))

    def spread(h, p):
        go(to_right[h][p])
        go(to_left[h][p])
        if is_direct[h][p]:
            go(hop2[h][p])

    def carry_on(h, p):
        if is_direct[h][p]:
            return
        got((to_right if rightward[h][p] else to_left)[h][p])
        go(onward[h][p])

    def rest(h, p):
        if is_direct[h][p]:
            got(to_left[h][p])
            got(to_right[h][p])
            got(hop2[h][p])
            return
        got((to_left if rightward[h][p] else to_right)[h][p])
        got(onward[h][p])

    over[0].start()
    spread(0, 0)
    spread(0, 1)
    spread(0, 2)
    for cp in loads[1:3]:
        cp.wait()
    lane = lax.broadcasted_iota(jnp.int32, (1, HEAD), 1)
    docs = doc[...]
    low = jnp.zeros((1, HEAD), jnp.float32)
    high = jnp.zeros((1, HEAD), jnp.float32)
    for d in range(4):
        under = jnp.sum((docs < d).astype(jnp.float32), axis=1, keepdims=True)
        upto = jnp.sum((docs <= d).astype(jnp.float32), axis=1, keepdims=True)
        low = jnp.where(lane == d, under, low)
        high = jnp.where(lane == d, upto, high)
    low = jnp.where(low >= GAP, low + (ROWS - TOK), low)
    high = jnp.where(high > GAP, high + (ROWS - TOK), high)
    row_at = lax.broadcasted_iota(jnp.int32, (ROWS, HEAD), 0).astype(jnp.float32)
    token = (row_at < GAP) | (row_at >= GAP + ROWS - TOK)
    inside = (row_at >= low) & (row_at < high) & token
    q_mark = jnp.where(inside, FAR, 0.0).astype(jnp.bfloat16)
    for h in range(HEADS):
        qbuf[h, :, 0:HEAD] = padded(qry[:, h * HEAD:(h + 1) * HEAD])
        qbuf[h, :, HEAD:2 * HEAD] = q_mark
    vx[:, HEAD:2 * HEAD] = jnp.ones((KEYS, HEAD), jnp.bfloat16)
    for cp in loads[3:]:
        cp.wait()

    over[0].wait_send()
    over[1].start()
    carry_on(0, 0)
    carry_on(0, 1)
    over[1].wait_send()
    go(over[2])
    carry_on(0, 2)
    got(over[0])
    spread(1, 0)

    whose = [(x * 2 + zh), ((x + 3) % 4) * 2 + zh, ((x + 1) % 4) * 2 + zh, ((x + 2) % 4) * 2 + zh]
    whose = whose + [w + 1 - 2 * zh for w in whose]

    def project(c):
        first, rows = CUT[c]
        part = jnp.zeros((rows, HEAD), jnp.float32)
        for slot in range(8):
            block = rbuf[slot, first:first + rows, :].astype(jnp.float32)
            term = (block - mean[whose[slot]]) * read[whose[slot]]
            for j in range(WIDTH // HEAD):
                part = part + term[:, j * HEAD:(j + 1) * HEAD]
        coef = jnp.sum(part, axis=1, keepdims=True)
        total = jnp.zeros((rows, 2 * HEAD), jnp.float32)
        for slot in range(8):
            block = rbuf[slot, first:first + rows, :].astype(jnp.float32)
            erased = (block - coef * drop[whose[slot]]).astype(jnp.bfloat16)
            weight = wbuf[pl.ds(pl.multiple_of(whose[slot] * WIDTH, WIDTH), WIDTH), :]
            total = total + jnp.dot(erased, weight, preferred_element_type=jnp.float32)
        if first == 0:
            at = lax.broadcasted_iota(jnp.int32, (rows, 2 * HEAD), 0)
            blank = jnp.zeros((1, HEAD), jnp.float32)
            low2 = jnp.concatenate([low, blank], axis=1)
            high2 = jnp.concatenate([high, blank], axis=1)
            total = jnp.where(at >= GAP, jnp.where(at == GAP, low2, jnp.where(at == GAP + 1, high2, 0.0)), total)
        kvbuf[OWN, first:first + rows, :] = total.astype(jnp.bfloat16)

    up = [copy(kvbuf, OWN, 0, cut, above) for cut in CUT]
    up2 = [copy(kvbuf, 0, 1, cut, above) for cut in CUT]
    near = [
        [copy(kvbuf, jnp.where(y + d < YN, OWN, 0), 4 * d, cut, ring(d)) for cut in CUT]
        for d in range(1, YN)
    ]
    far = [[copy(kvbuf, 4 * d, 4 * d + 1, cut, above) for cut in CUT] for d in range(1, YN)]
    side = [copy(kvbuf, OWN, MATE, cut, mate) for cut in CUT]

    def pair(d, c):
        i = used[0]
        used[0] += 1
        first, rows = CUT[c]
        return pltpu.make_async_remote_copy(
            src_ref=kvbuf.at[pl.ds(4 * d, 2), pl.ds(first, rows)],
            dst_ref=kvbuf.at[pl.ds(4 * d + 2, 2), pl.ds(first, rows)],
            send_sem=ssem.at[i],
            recv_sem=rsem.at[i],
            device_id=mate,
            device_id_type=MESH,
        )

    pairs = [[pair(d, c) for c in range(len(CUT))] for d in range(YN)]
    order = sorted(range(1, YN), key=lambda d: min(d, YN - d))

    def share(c):
        go(up[c], has_above)
        for d in order:
            go(near[d - 1][c], y + d < YN)
        go(side[c], core == 0)

    def wrapped(c):
        got(up[c], has_below)
        go(up2[c], has_above)
        for d in order:
            go(near[d - 1][c], y + d >= YN)

    def relay(c, d):
        got(near[d - 1][c])
        go(far[d - 1][c], has_above)

    def attend(blocks, start=False, own=False):
        keys = sum(rows for _, (_, rows) in blocks)
        at = 0
        for slot, (first, rows) in blocks:
            put = slice(at, at + rows)
            at += rows
            block = kvbuf[slot, first:first + rows, :]
            kx[put, 0:HEAD] = block[:, 0:HEAD]
            vx[put, 0:HEAD] = block[:, HEAD:2 * HEAD]
            mark = kvbuf[slot, GAP - 8:GAP + 8, 0:HEAD].astype(jnp.float32)
            here = slice(first, first + rows)
            seen = (row_at[here] >= mark[8:9]) & (row_at[here] < mark[9:10]) & token[here]
            kx[put, HEAD:2 * HEAD] = jnp.where(seen, 0.0, 1.0).astype(jnp.bfloat16)

        score = lax.dot_general(
            qbuf[...].reshape(HEADS * ROWS, 2 * HEAD), kx[0:keys], (((1,), (1,)), ((), ())),
            preferred_element_type=jnp.float32,
        )
        if own:
            shape = (HEADS, ROWS, keys)
            q_at = lax.broadcasted_iota(jnp.int32, shape, 1).reshape(HEADS * ROWS, keys)
            k_at = lax.broadcasted_iota(jnp.int32, shape, 2).reshape(HEADS * ROWS, keys)
            score = jnp.where((k_at <= q_at) | (k_at >= ROWS), score, FAR)
        cuts = [score[:, i:i + HEAD] for i in range(0, keys, HEAD)]
        whole = [tile for tile in cuts if tile.shape[1] == HEAD]
        rough = functools.reduce(jnp.maximum, whole)
        best = jnp.max(rough, axis=1, keepdims=True)
        if len(whole) < len(cuts):
            best = jnp.maximum(best, jnp.max(cuts[-1], axis=1, keepdims=True))
        best = jnp.broadcast_to(best, (HEADS * ROWS, HEAD))
        if not start:
            old = top[...]
            best = jnp.maximum(best, old)
        wide = jnp.concatenate([best[:, :tile.shape[1]] for tile in cuts], axis=1)
        expo = jnp.exp2((score - wide) * (SCALE * LOG2E)).astype(jnp.bfloat16)
        mixed = jnp.dot(expo, vx[0:keys], preferred_element_type=jnp.float32)
        if not start:
            factor = jnp.exp2((old - best) * (SCALE * LOG2E))
            mixed = mixed + acc[...] * jnp.concatenate([factor, factor], axis=1)
        acc[...] = mixed
        top[...] = best

    pool = [0] + order

    def to_mate(c, *groups):
        for d in groups:
            if d == 0:
                got(up2[c], has_below)
            else:
                got(far[d - 1][c], has_below)
            go(pairs[d][c])

    def take(c, *groups, start=False):
        for d in groups:
            got(pairs[d][c])
        attend([(4 * d + j, CUT[c]) for d in groups for j in range(4)], start)

    def relays(c, *groups):
        for d in groups:
            relay(c, d)

    carry_on(1, 0)
    got(over[1])
    spread(1, 1)
    rest(0, 0)
    rest(1, 0)
    project(0)
    share(0)
    carry_on(1, 1)
    got(over[2])
    spread(1, 2)
    wrapped(0)
    rest(0, 1)
    rest(1, 1)
    project(1)
    share(1)
    carry_on(1, 2)
    relays(0, *order)
    to_mate(0, *pool[:4])
    wrapped(1)
    rest(0, 2)
    rest(1, 2)
    project(2)
    share(2)
    to_mate(0, *pool[4:])
    take(0, *pool[0:2], start=True)
    relays(1, *order[:3])
    take(0, *pool[2:4])
    wrapped(2)
    relays(1, *order[3:])
    take(0, *pool[4:6])
    to_mate(1, *pool[:4])
    take(0, *pool[6:8])
    relays(2, *order[:3])
    to_mate(1, *pool[4:])
    for c in range(3):
        got(side[c], core == 1)
    attend([(OWN, (0, ROWS)), (MATE, (0, ROWS))], own=True)
    relays(2, *order[3:])
    take(1, *pool[:4])
    to_mate(2, *pool[:4])
    take(1, *pool[4:])
    to_mate(2, *pool[4:])
    take(2, *pool[:4])
    take(2, *pool[4:])

    for h in range(HEADS):
        both = acc[h * ROWS:(h + 1) * ROWS]
        mean_value = (both[:, 0:HEAD] / both[:, HEAD:2 * HEAD])
        kept = jnp.concatenate([mean_value[:GAP], mean_value[GAP + ROWS - TOK:]], axis=0)
        out[:, h * HEAD:(h + 1) * HEAD] = kept.astype(jnp.bfloat16)

    for cp, when in sent:
        if when is None:
            cp.wait_send()
        else:
            pl.when(when)(cp.wait_send)


def on_device(residual, mean_vec, proj_u, proj_v, key_weight, value_weight, queries, doc_ids):
    whole = pl.BlockSpec(memory_space=pltpu.VMEM)
    hbm = pl.BlockSpec(memory_space=pltpu.HBM)
    flat = (8, 1, WIDTH)
    return pl.pallas_call(
        kernel,
        out_shape=jax.ShapeDtypeStruct((TOK, WIDTH), jnp.bfloat16),
        in_specs=[hbm] * 8,
        out_specs=whole,
        scratch_shapes=[
            pltpu.VMEM((TOK, WIDTH), jnp.bfloat16),
            pltpu.VMEM(flat, jnp.float32),
            pltpu.VMEM(flat, jnp.float32),
            pltpu.VMEM(flat, jnp.float32),
            pltpu.VMEM((TOK, WIDTH), jnp.bfloat16),
            pltpu.VMEM((1, TOK), jnp.int32),
            pltpu.VMEM((8, ROWS, WIDTH), jnp.bfloat16),
            pltpu.VMEM((8 * WIDTH, 2 * HEAD), jnp.bfloat16),
            pltpu.VMEM((SLOTS, ROWS, 2 * HEAD), jnp.bfloat16),
            pltpu.VMEM((HEADS, ROWS, 2 * HEAD), jnp.bfloat16),
            pltpu.VMEM((KEYS, 2 * HEAD), jnp.bfloat16),
            pltpu.VMEM((KEYS, 2 * HEAD), jnp.bfloat16),
            pltpu.VMEM((HEADS * ROWS, 2 * HEAD), jnp.float32),
            pltpu.VMEM((HEADS * ROWS, HEAD), jnp.float32),
            pltpu.SemaphoreType.DMA((SEMS,)),
            pltpu.SemaphoreType.DMA((SEMS,)),
            pltpu.SemaphoreType.DMA((8,)),
        ],
        compiler_params=pltpu.CompilerParams(
            collective_id=0, has_side_effects=True, vmem_limit_bytes=60 << 20
        ),
    )(
        residual, mean_vec.reshape(flat), proj_u.reshape(flat), proj_v.reshape(flat),
        key_weight, value_weight, queries, doc_ids.reshape(1, TOK),
    )


def solution(mesh):
    return jax.shard_map(
        on_device,
        mesh=mesh,
        in_specs=(
            P("seq", "tensor"), P(), P(), P(), P(None, "tensor"), P(None, "tensor"),
            P("seq", "tensor"), P("seq"),
        ),
        out_specs=P("seq", "tensor"),
        check_vma=False,
    )
```

```python
import functools
import jax
import jax.numpy as jnp
from jax import lax
from jax.experimental import pallas as pl
from jax.experimental.pallas import tpu as pltpu
from jax.sharding import PartitionSpec as P

HEADS = 8
HEAD = 128
TOK = 152
ROWS = 160
GAP = 40
CUT = ((0, 48), (48, 64), (112, 48))
WIDTH = 1024
YN = 8
SCALE = 1.0 / HEAD**0.5
LOG2E = 1.4426950408889634
FAR = -1e30
MESH = pl.DeviceIdType.MESH
OWN, MATE = 4 * YN, 4 * YN + 1
SLOTS = 4 * YN + 2
SEMS = 112
KEYS = 1024


def kernel(
    res_hbm, mean_hbm, read_hbm, drop_hbm, wk_hbm, wv_hbm, qry_hbm, doc_hbm, out,
    res, mean, read, drop, qry, doc,
    rbuf, wbuf, kvbuf, qbuf, kx, vx, acc, top, ssem, rsem, wsem,
):
    t = lax.axis_index("tensor")
    s = lax.axis_index("seq")
    x, zh = t // 2, t % 2
    zl, y, core = s // 16, (s // 2) % YN, s % 2

    def dev(x_, zh_, zl_, y_, core_):
        return (x_ * 2 + zh_, zl_ * 16 + y_ * 2 + core_)

    right = dev((x + 1) % 4, zh, zl, y, core)
    left = dev((x + 3) % 4, zh, zl, y, core)
    facing = dev((x + 2) % 4, zh, zl, y, core)
    across = dev(x, 1 - zh, zl, y, core)
    above = dev(x, zh, (zl + 1) % 4, y, core)
    below = dev(x, zh, (zl + 3) % 4, y, core)
    mate = dev(x, zh, zl, y, 1 - core)
    has_above, has_below = zl < 3, zl > 0

    def ring(d):
        return dev(x, zh, zl, (y + d) % YN, core)

    bar = pltpu.get_barrier_semaphore()

    def hello(device):
        pl.semaphore_signal(bar, inc=1, device_id=device, device_id_type=MESH)

    for device in [right, left, facing, across, mate] + [ring(d) for d in range(1, YN)]:
        hello(device)

    @pl.when(has_above)
    def _():
        hello(above)

    @pl.when(has_below)
    def _():
        hello(below)

    loads = [
        pltpu.make_async_copy(src, dst, wsem.at[i])
        for i, (src, dst) in enumerate([
            (res_hbm, res), (doc_hbm, doc), (qry_hbm, qry), (mean_hbm, mean), (read_hbm, read), (drop_hbm, drop),
            (wk_hbm, wbuf.at[:, pl.ds(0, HEAD)]), (wv_hbm, wbuf.at[:, pl.ds(HEAD, HEAD)]),
        ])
    ]
    for cp in loads:
        cp.start()

    def padded(value):
        wide = value.astype(jnp.float32)
        blank = jnp.zeros((ROWS - TOK, wide.shape[1]), jnp.float32)
        return jnp.concatenate([wide[:GAP], blank, wide[GAP:]], axis=0).astype(jnp.bfloat16)

    empty = jnp.zeros((ROWS, 2 * HEAD), jnp.bfloat16)

    @pl.when(core == 0)
    def _():
        kvbuf[MATE] = empty

    @pl.when(zl == 0)
    def _():
        kvbuf[0] = empty
        for d in range(YN):
            kvbuf[4 * d + 1] = empty

    loads[0].wait()
    rbuf[0] = padded(res[...])

    peers = 5 + YN - 1 + jnp.where(has_above, 1, 0) + jnp.where(has_below, 1, 0)
    pl.semaphore_wait(bar, peers)

    used = [0]
    sent = []

    def copy(buf, src, dst, cut, device):
        i = used[0]
        used[0] += 1
        first, rows = cut
        return pltpu.make_async_remote_copy(
            src_ref=buf.at[src, pl.ds(first, rows)],
            dst_ref=buf.at[dst, pl.ds(first, rows)],
            send_sem=ssem.at[i],
            recv_sem=rsem.at[i],
            device_id=device,
            device_id_type=MESH,
        )

    def go(cp, when=None):
        sent.append((cp, when))
        if when is None:
            cp.start()
        else:
            pl.when(when)(cp.start)

    def got(cp, when=None):
        if when is None:
            cp.wait_recv()
        else:
            pl.when(when)(cp.wait_recv)

    over = [copy(rbuf, 0, 4, cut, across) for cut in CUT]
    to_right = [[copy(rbuf, 4 * h, 4 * h + 1, cut, right) for cut in CUT] for h in range(2)]
    to_left = [[copy(rbuf, 4 * h, 4 * h + 2, cut, left) for cut in CUT] for h in range(2)]
    rightward = ((True, False, False), (False, True, True))
    onward = [
        [
            copy(rbuf, 4 * h + 1, 4 * h + 3, cut, right) if way else copy(rbuf, 4 * h + 2, 4 * h + 3, cut, left)
            for way, cut in zip(rightward[h], CUT)
        ]
        for h in range(2)
    ]

    hop2 = [[copy(rbuf, 4 * h, 4 * h + 3, cut, facing) for cut in CUT] for h in range(2)]
    is_direct = ((False, False, False), (True, True, True))

    def spread(h, p):
        go(to_right[h][p])
        go(to_left[h][p])
        if is_direct[h][p]:
            go(hop2[h][p])

    def carry_on(h, p):
        if is_direct[h][p]:
            return
        got((to_right if rightward[h][p] else to_left)[h][p])
        go(onward[h][p])

    def rest(h, p):
        if is_direct[h][p]:
            got(to_left[h][p])
            got(to_right[h][p])
            got(hop2[h][p])
            return
        got((to_left if rightward[h][p] else to_right)[h][p])
        got(onward[h][p])

    over[0].start()
    spread(0, 0)
    spread(0, 1)
    spread(0, 2)
    for cp in loads[1:3]:
        cp.wait()
    lane = lax.broadcasted_iota(jnp.int32, (1, HEAD), 1)
    docs = doc[...]
    low = jnp.zeros((1, HEAD), jnp.float32)
    high = jnp.zeros((1, HEAD), jnp.float32)
    for d in range(4):
        under = jnp.sum((docs < d).astype(jnp.float32), axis=1, keepdims=True)
        upto = jnp.sum((docs <= d).astype(jnp.float32), axis=1, keepdims=True)
        low = jnp.where(lane == d, under, low)
        high = jnp.where(lane == d, upto, high)
    low = jnp.where(low >= GAP, low + (ROWS - TOK), low)
    high = jnp.where(high > GAP, high + (ROWS - TOK), high)
    row_at = lax.broadcasted_iota(jnp.int32, (ROWS, HEAD), 0).astype(jnp.float32)
    token = (row_at < GAP) | (row_at >= GAP + ROWS - TOK)
    inside = (row_at >= low) & (row_at < high) & token
    q_mark = jnp.where(inside, FAR, 0.0).astype(jnp.bfloat16)
    for h in range(HEADS):
        qbuf[h, :, 0:HEAD] = padded(qry[:, h * HEAD:(h + 1) * HEAD])
        qbuf[h, :, HEAD:2 * HEAD] = q_mark
    vx[:, HEAD:2 * HEAD] = jnp.ones((KEYS, HEAD), jnp.bfloat16)
    for cp in loads[3:]:
        cp.wait()

    over[0].wait_send()
    over[1].start()
    carry_on(0, 0)
    carry_on(0, 1)
    over[1].wait_send()
    go(over[2])
    carry_on(0, 2)
    got(over[0])
    spread(1, 0)

    whose = [(x * 2 + zh), ((x + 3) % 4) * 2 + zh, ((x + 1) % 4) * 2 + zh, ((x + 2) % 4) * 2 + zh]
    whose = whose + [w + 1 - 2 * zh for w in whose]

    def project(c):
        first, rows = CUT[c]
        part = jnp.zeros((rows, HEAD), jnp.float32)
        for slot in range(8):
            block = rbuf[slot, first:first + rows, :].astype(jnp.float32)
            term = (block - mean[whose[slot]]) * read[whose[slot]]
            for j in range(WIDTH // HEAD):
                part = part + term[:, j * HEAD:(j + 1) * HEAD]
        coef = jnp.sum(part, axis=1, keepdims=True)
        total = jnp.zeros((rows, 2 * HEAD), jnp.float32)
        for slot in range(8):
            block = rbuf[slot, first:first + rows, :].astype(jnp.float32)
            erased = (block - coef * drop[whose[slot]]).astype(jnp.bfloat16)
            weight = wbuf[pl.ds(pl.multiple_of(whose[slot] * WIDTH, WIDTH), WIDTH), :]
            total = total + jnp.dot(erased, weight, preferred_element_type=jnp.float32)
        if first == 0:
            at = lax.broadcasted_iota(jnp.int32, (rows, 2 * HEAD), 0)
            blank = jnp.zeros((1, HEAD), jnp.float32)
            low2 = jnp.concatenate([low, blank], axis=1)
            high2 = jnp.concatenate([high, blank], axis=1)
            total = jnp.where(at >= GAP, jnp.where(at == GAP, low2, jnp.where(at == GAP + 1, high2, 0.0)), total)
        kvbuf[OWN, first:first + rows, :] = total.astype(jnp.bfloat16)

    up = [copy(kvbuf, OWN, 0, cut, above) for cut in CUT]
    up2 = [copy(kvbuf, 0, 1, cut, above) for cut in CUT]
    near = [
        [copy(kvbuf, jnp.where(y + d < YN, OWN, 0), 4 * d, cut, ring(d)) for cut in CUT]
        for d in range(1, YN)
    ]
    far = [[copy(kvbuf, 4 * d, 4 * d + 1, cut, above) for cut in CUT] for d in range(1, YN)]
    side = [copy(kvbuf, OWN, MATE, cut, mate) for cut in CUT]

    def pair(d, c):
        i = used[0]
        used[0] += 1
        first, rows = CUT[c]
        return pltpu.make_async_remote_copy(
            src_ref=kvbuf.at[pl.ds(4 * d, 2), pl.ds(first, rows)],
            dst_ref=kvbuf.at[pl.ds(4 * d + 2, 2), pl.ds(first, rows)],
            send_sem=ssem.at[i],
            recv_sem=rsem.at[i],
            device_id=mate,
            device_id_type=MESH,
        )

    pairs = [[pair(d, c) for c in range(len(CUT))] for d in range(YN)]
    order = sorted(range(1, YN), key=lambda d: min(d, YN - d))

    def share(c):
        go(up[c], has_above)
        for d in order:
            go(near[d - 1][c], y + d < YN)
        go(side[c], core == 0)

    def wrapped(c):
        got(up[c], has_below)
        go(up2[c], has_above)
        for d in order:
            go(near[d - 1][c], y + d >= YN)

    def relay(c, d):
        got(near[d - 1][c])
        go(far[d - 1][c], has_above)

    def attend(blocks, start=False, own=False):
        keys = sum(rows for _, (_, rows) in blocks)
        at = 0
        for slot, (first, rows) in blocks:
            put = slice(at, at + rows)
            at += rows
            block = kvbuf[slot, first:first + rows, :]
            kx[put, 0:HEAD] = block[:, 0:HEAD]
            vx[put, 0:HEAD] = block[:, HEAD:2 * HEAD]
            mark = kvbuf[slot, GAP - 8:GAP + 8, 0:HEAD].astype(jnp.float32)
            here = slice(first, first + rows)
            seen = (row_at[here] >= mark[8:9]) & (row_at[here] < mark[9:10]) & token[here]
            kx[put, HEAD:2 * HEAD] = jnp.where(seen, 0.0, 1.0).astype(jnp.bfloat16)

        score = lax.dot_general(
            qbuf[...].reshape(HEADS * ROWS, 2 * HEAD), kx[0:keys], (((1,), (1,)), ((), ())),
            preferred_element_type=jnp.float32,
        )
        if own:
            shape = (HEADS, ROWS, keys)
            q_at = lax.broadcasted_iota(jnp.int32, shape, 1).reshape(HEADS * ROWS, keys)
            k_at = lax.broadcasted_iota(jnp.int32, shape, 2).reshape(HEADS * ROWS, keys)
            score = jnp.where((k_at <= q_at) | (k_at >= ROWS), score, FAR)
        cuts = [score[:, i:i + HEAD] for i in range(0, keys, HEAD)]
        whole = [tile for tile in cuts if tile.shape[1] == HEAD]
        rough = functools.reduce(jnp.maximum, whole)
        best = jnp.max(rough, axis=1, keepdims=True)
        if len(whole) < len(cuts):
            best = jnp.maximum(best, jnp.max(cuts[-1], axis=1, keepdims=True))
        best = jnp.broadcast_to(best, (HEADS * ROWS, HEAD))
        if not start:
            old = top[...]
            best = jnp.maximum(best, old)
        wide = jnp.concatenate([best[:, :tile.shape[1]] for tile in cuts], axis=1)
        expo = jnp.exp2((score - wide) * (SCALE * LOG2E)).astype(jnp.bfloat16)
        mixed = jnp.dot(expo, vx[0:keys], preferred_element_type=jnp.float32)
        if not start:
            factor = jnp.exp2((old - best) * (SCALE * LOG2E))
            mixed = mixed + acc[...] * jnp.concatenate([factor, factor], axis=1)
        acc[...] = mixed
        top[...] = best

    pool = [0] + order

    def to_mate(c, *groups):
        for d in groups:
            if d == 0:
                got(up2[c], has_below)
            else:
                got(far[d - 1][c], has_below)
            go(pairs[d][c])

    def take(c, *groups, start=False):
        for d in groups:
            got(pairs[d][c])
        attend([(4 * d + j, CUT[c]) for d in groups for j in range(4)], start)

    def relays(c, *groups):
        for d in groups:
            relay(c, d)

    carry_on(1, 0)
    got(over[1])
    spread(1, 1)
    rest(0, 0)
    rest(1, 0)
    project(0)
    share(0)
    carry_on(1, 1)
    got(over[2])
    spread(1, 2)
    wrapped(0)
    rest(0, 1)
    rest(1, 1)
    project(1)
    share(1)
    carry_on(1, 2)
    relays(0, *order)
    to_mate(0, *pool[:4])
    wrapped(1)
    rest(0, 2)
    rest(1, 2)
    project(2)
    share(2)
    to_mate(0, *pool[4:])
    take(0, *pool[0:4], start=True)
    relays(1, *order)
    wrapped(2)
    take(0, *pool[4:8])
    to_mate(1, *pool[:4])
    relays(2, *order[:3])
    to_mate(1, *pool[4:])
    for c in range(3):
        got(side[c], core == 1)
    attend([(OWN, (0, ROWS)), (MATE, (0, ROWS))], own=True)
    relays(2, *order[3:])
    take(1, *pool[:4])
    to_mate(2, *pool[:4])
    take(1, *pool[4:])
    to_mate(2, *pool[4:])
    take(2, *pool[:4])
    take(2, *pool[4:])

    for h in range(HEADS):
        both = acc[h * ROWS:(h + 1) * ROWS]
        mean_value = (both[:, 0:HEAD] / both[:, HEAD:2 * HEAD])
        kept = jnp.concatenate([mean_value[:GAP], mean_value[GAP + ROWS - TOK:]], axis=0)
        out[:, h * HEAD:(h + 1) * HEAD] = kept.astype(jnp.bfloat16)

    for cp, when in sent:
        if when is None:
            cp.wait_send()
        else:
            pl.when(when)(cp.wait_send)


def on_device(residual, mean_vec, proj_u, proj_v, key_weight, value_weight, queries, doc_ids):
    whole = pl.BlockSpec(memory_space=pltpu.VMEM)
    hbm = pl.BlockSpec(memory_space=pltpu.HBM)
    flat = (8, 1, WIDTH)
    return pl.pallas_call(
        kernel,
        out_shape=jax.ShapeDtypeStruct((TOK, WIDTH), jnp.bfloat16),
        in_specs=[hbm] * 8,
        out_specs=whole,
        scratch_shapes=[
            pltpu.VMEM((TOK, WIDTH), jnp.bfloat16),
            pltpu.VMEM(flat, jnp.float32),
            pltpu.VMEM(flat, jnp.float32),
            pltpu.VMEM(flat, jnp.float32),
            pltpu.VMEM((TOK, WIDTH), jnp.bfloat16),
            pltpu.VMEM((1, TOK), jnp.int32),
            pltpu.VMEM((8, ROWS, WIDTH), jnp.bfloat16),
            pltpu.VMEM((8 * WIDTH, 2 * HEAD), jnp.bfloat16),
            pltpu.VMEM((SLOTS, ROWS, 2 * HEAD), jnp.bfloat16),
            pltpu.VMEM((HEADS, ROWS, 2 * HEAD), jnp.bfloat16),
            pltpu.VMEM((KEYS, 2 * HEAD), jnp.bfloat16),
            pltpu.VMEM((KEYS, 2 * HEAD), jnp.bfloat16),
            pltpu.VMEM((HEADS * ROWS, 2 * HEAD), jnp.float32),
            pltpu.VMEM((HEADS * ROWS, HEAD), jnp.float32),
            pltpu.SemaphoreType.DMA((SEMS,)),
            pltpu.SemaphoreType.DMA((SEMS,)),
            pltpu.SemaphoreType.DMA((8,)),
        ],
        compiler_params=pltpu.CompilerParams(
            collective_id=0, has_side_effects=True, vmem_limit_bytes=60 << 20
        ),
    )(
        residual, mean_vec.reshape(flat), proj_u.reshape(flat), proj_v.reshape(flat),
        key_weight, value_weight, queries, doc_ids.reshape(1, TOK),
    )


def solution(mesh):
    return jax.shard_map(
        on_device,
        mesh=mesh,
        in_specs=(
            P("seq", "tensor"), P(), P(), P(), P(None, "tensor"), P(None, "tensor"),
            P("seq", "tensor"), P("seq"),
        ),
        out_specs=P("seq", "tensor"),
        check_vma=False,
    )
```
